256 devices in a mesh: fsdp: 64 (over z, x, y_lo), tensor: 4 (over y_hi, core).
Axes of the slice: x: 4, y: 4 (y_hi: 2, y_lo: 2; y = y_hi * 2 + y_lo), z: 8, core: 2. Of those that a mesh axis runs over, the one named last changes fastest.
Arguments:
- tokens: bfloat16 [512, 8192], P('fsdp', 'tensor'), may hold values from -6 to 6
- gate_weight: bfloat16 [8192, 28672], P('tensor', 'fsdp'), may hold values from -0.125 to 0.125
- up_weight: bfloat16 [8192, 28672], P('tensor', 'fsdp'), may hold values from -0.125 to 0.125
- down_weight: bfloat16 [28672, 8192], P('fsdp', 'tensor'), may hold values from -0.0625 to 0.0625
- gate_mask: int32 [64, 64], replicated, may hold values from 0 to 1, as said below
- up_mask: int32 [64, 64], replicated, may hold values from 0 to 1, as said below
- down_mask: int32 [64, 64], replicated, may hold values from 0 to 1, as said below
- cotangent: bfloat16 [512, 8192], P('fsdp', 'tensor'), may hold values from -6 to 6
Outputs:
- ffn_output: bfloat16 [512, 8192], P('fsdp', 'tensor')
- grad_tokens: bfloat16 [512, 8192], P('fsdp', 'tensor')
- grad_gate: bfloat16 [8192, 28672], P('tensor', 'fsdp')
- grad_up: bfloat16 [8192, 28672], P('tensor', 'fsdp')
- grad_down: bfloat16 [28672, 8192], P('fsdp', 'tensor')
The draws below stay inside these ranges and needn't reach their ends.
Inputs may be any that keep to these rules, and one draw needn't show every extreme that they name: `gate_mask`: entries are 0 or 1. For every hidden block c and every group of 16 consecutive width blocks, between 1 and 8 of the entries pairing c with the group are 1, and exactly 8 for every group of some hidden block in every draw. Counts differ from one hidden block to another. `up_mask`: as for gate_mask, with its own pattern. `down_mask`: entries are 0 or 1. For every hidden block c (row) and every group of 16 consecutive width blocks (columns), between 1 and 8 of the entries are 1, and exactly 8 for every group of some hidden block in every draw. Counts differ from one hidden block to another.
All inputs are finite; a program needn't handle non-finite values.
Results may differ from the reference program's by a relative error of at most 0.005.
Values may be sent and summed in bfloat16 or wider, within the bound.
No kernel may reach another device: no remote copies, remote signals or barrier semaphores. Data moves between devices by JAX's collectives and lax.ppermute only.
A program may use at most 64 MiB of HBM per device.

```python
import jax
import jax.numpy as jnp
from jax import lax

D = 8192
FF = 28672
NBLK = 64
KMAX = 8
TOKENS = 512
GROUP = 16


def block_layout(key):
    groups = NBLK // GROUP
    key_heavy, key_base, key_rank, key_pick = jax.random.split(key, 4)
    base_count = jax.random.randint(key_base, (NBLK, groups), 1, 6)
    heavy_block = jax.random.randint(key_heavy, (NBLK, 1), 0, 4) == 0
    forced = jax.random.permutation(key_pick, NBLK)[0]
    heavy_block = heavy_block | (lax.broadcasted_iota(jnp.int32, (NBLK, 1), 0) == forced)
    counts = jnp.where(heavy_block, KMAX, jnp.minimum(base_count, KMAX))
    scores = jax.random.randint(key_rank, (NBLK, groups, GROUP), 0, 1 << 20) * GROUP + lax.broadcasted_iota(jnp.int32, (NBLK, groups, GROUP), 2)
    ranking = jnp.argsort(jnp.argsort(scores, axis=2), axis=2)
    return (ranking < counts[:, :, None]).astype(jnp.int32).reshape(NBLK, NBLK)


def draw_gate_mask(key, part):
    key = jax.random.fold_in(key, 11)
    return block_layout(key).T


def draw_up_mask(key, part):
    key = jax.random.fold_in(key, 12)
    return block_layout(key).T


def draw_down_mask(key, part):
    key = jax.random.fold_in(key, 13)
    return block_layout(key)


def shard_levels(own_key, extent, cuts, low, top_value):
    def one(dim, blocks):
        heights = jax.random.uniform(jax.random.fold_in(jax.random.fold_in(own_key, 6), dim), (blocks,), jnp.float32, low / len(cuts), top_value / len(cuts))
        return jnp.repeat(jnp.exp(heights), extent[dim] // blocks).reshape((-1,) + (1,) * (len(extent) - dim - 1))

    gain = one(*cuts[0])
    for cut in cuts[1:]:
        gain = gain * one(*cut)
    return gain


def scatter_about(key, shape, spread, limit, cuts=(), kind=jnp.bfloat16):
    factor_of = shard_levels(key, shape, cuts, -0.22, 0.18) if cuts else 1.0
    array = jax.random.normal(key, shape, jnp.float32) * spread * factor_of
    return jnp.minimum(jnp.maximum(array, -limit), limit).astype(kind)


def setup_inputs(seed: int = 0) -> dict:
    keys = jax.random.split(jax.random.key(seed), 9)
    return {
        "tokens": scatter_about(keys[0], (TOKENS, D), 1.0, 6.0, ((0, 64), (1, 4))),
        "gate_weight": scatter_about(keys[1], (D, FF), (D // 4) ** -0.5, 0.125, ((0, 4), (1, 64))),
        "up_weight": scatter_about(keys[2], (D, FF), (D // 4) ** -0.5, 0.125, ((0, 4), (1, 64))),
        "down_weight": scatter_about(keys[3], (FF, D), (FF // 4) ** -0.5, 0.0625, ((0, 64), (1, 4))),
        "gate_mask": draw_gate_mask(jax.random.fold_in(keys[8], 71), 0),
        "up_mask": draw_up_mask(jax.random.fold_in(keys[8], 71), 0),
        "down_mask": draw_down_mask(jax.random.fold_in(keys[8], 71), 0),
        "cotangent": scatter_about(keys[7], (TOKENS, D), 1.0, 6.0, ((0, 64), (1, 4))),
    }


def reference(tokens, gate_weight, up_weight, down_weight, gate_mask, up_mask, down_mask, cotangent):
    d_tile = D // NBLK
    f_tile = FF // NBLK
    rows_total = tokens.shape[0]
    gate_cols = gate_weight.reshape(D, NBLK, f_tile).transpose(1, 0, 2)
    up_cols = up_weight.reshape(D, NBLK, f_tile).transpose(1, 0, 2)
    down_rows = down_weight.reshape(NBLK, f_tile, D)

    def step_block(carry, pieces):
        output_acc, input_acc = carry
        gate_block, up_block, down_block, gate_on, up_on, down_on = pieces
        gate_scale = jnp.repeat(gate_on, d_tile)[:, None]
        up_scale = jnp.repeat(up_on, d_tile)[:, None]
        down_scale = jnp.repeat(down_on, d_tile)[None, :]
        gate_masked = gate_block * gate_scale.astype(gate_block.dtype)
        up_masked = up_block * up_scale.astype(up_block.dtype)
        down_masked = down_block * down_scale.astype(down_block.dtype)
        gate_sum = jnp.dot(tokens, gate_masked, preferred_element_type=jnp.float32)
        up_sum = jnp.dot(tokens, up_masked, preferred_element_type=jnp.float32)
        sigmoid_gate = jax.nn.sigmoid(gate_sum)
        silu_gate = gate_sum * sigmoid_gate
        hidden = (silu_gate * up_sum).astype(jnp.bfloat16)
        output_acc = output_acc + jnp.dot(hidden, down_masked, preferred_element_type=jnp.float32)
        back_sum = jnp.dot(cotangent, down_masked.T, preferred_element_type=jnp.float32)
        grad_gate_act = (back_sum * up_sum * sigmoid_gate * (1.0 + gate_sum * (1.0 - sigmoid_gate))).astype(jnp.bfloat16)
        grad_up_act = (back_sum * silu_gate).astype(jnp.bfloat16)
        grad_down_block = (jnp.dot(hidden.T, cotangent, preferred_element_type=jnp.float32) * down_scale.astype(jnp.float32)).astype(jnp.bfloat16)
        grad_gate_block = (jnp.dot(tokens.T, grad_gate_act, preferred_element_type=jnp.float32) * gate_scale.astype(jnp.float32)).astype(jnp.bfloat16)
        grad_up_block = (jnp.dot(tokens.T, grad_up_act, preferred_element_type=jnp.float32) * up_scale.astype(jnp.float32)).astype(jnp.bfloat16)
        input_acc = input_acc + jnp.dot(grad_gate_act, gate_masked.T, preferred_element_type=jnp.float32) + jnp.dot(grad_up_act, up_masked.T, preferred_element_type=jnp.float32)
        return (output_acc, input_acc), (grad_gate_block, grad_up_block, grad_down_block)

    start_acc = jnp.zeros((rows_total, D), jnp.float32)
    carried, stacked = lax.scan(step_block, (start_acc, start_acc), (gate_cols, up_cols, down_rows, gate_mask.T, up_mask.T, down_mask))
    output_acc, input_acc = carried
    grad_gate = stacked[0].transpose(1, 0, 2).reshape(D, FF)
    grad_up = stacked[1].transpose(1, 0, 2).reshape(D, FF)
    grad_down = stacked[2].reshape(FF, D)
    return (output_acc.astype(jnp.bfloat16), input_acc.astype(jnp.bfloat16), grad_gate, grad_up, grad_down)
```

```python
import functools
import jax
import jax.numpy as jnp
from jax import lax
from jax.experimental import pallas as pl
from jax.experimental.pallas import tpu as pltpu
from jax.sharding import PartitionSpec as P

NZ, NX, NY = 8, 4, 2
NBLK, GROUP, KMAX = 64, 16, 8
DT, FT = 128, 448
W = GROUP * DT
PK = KMAX * DT
T = 512
BF, F32 = jnp.bfloat16, jnp.float32
VMEM = pl.BlockSpec(memory_space=pltpu.VMEM)
SMEM = pl.BlockSpec(memory_space=pltpu.SMEM)


def fsdp_perm(dz, dx, dy):
    pairs = []
    for z in range(NZ):
        for x in range(NX):
            for y in range(NY):
                src = (z * NX + x) * NY + y
                dst = ((z + dz) % NZ * NX + (x + dx) % NX) * NY + (y + dy) % NY
                pairs.append((src, dst))
    return pairs


def shift(v, dz=0, dx=0, dy=0):
    return lax.ppermute(v, "fsdp", fsdp_perm(dz, dx, dy))


def swap_core(v):
    return lax.ppermute(v, "tensor", [(i, i ^ 1) for i in range(4)])


def swap_far(v):
    return lax.ppermute(v, "tensor", [(i, i ^ 2) for i in range(4)])


def call(body, outs, in_specs, out_specs, scratch=(), flops=0, moved=0):
    return pl.pallas_call(
        body,
        out_shape=outs,
        in_specs=in_specs,
        out_specs=out_specs,
        scratch_shapes=list(scratch),
        compiler_params=pltpu.CompilerParams(vmem_limit_bytes=40 * 1024 * 1024),
        cost_estimate=pl.CostEstimate(flops=flops, bytes_accessed=moved, transcendentals=0),
    )


def sds(shape, dtype):
    return jax.ShapeDtypeStruct(shape, dtype)


def slot(order, row, k):
    return pl.ds(pl.multiple_of(order[row, k] * DT, DT), DT)


def prep_body(meta, gm, um, dm, gw, uw, dw, order, pg, pu, pd):
    z, x, y, t = meta[0], meta[1], meta[2], meta[3]
    for row in range(6):
        fx = lax.rem(x + row, NX) if row < 4 else x
        f = (z * NX + fx) * NY + y
        for k in range(GROUP + 1):
            order[row, k] = 0
        n = jnp.int32(0)
        for j in range(GROUP):
            if row < 4:
                m = dm[f, t * GROUP + j]
            elif row == 4:
                m = gm[t * GROUP + j, f]
            else:
                m = um[t * GROUP + j, f]
            order[row, n] = j
            n = n + m
        order[row, GROUP] = n
    for k in range(KMAX):
        here = slice(k * DT, (k + 1) * DT)
        for row, src, dst in ((4, gw, pg), (5, uw, pu)):
            @pl.when(k < order[row, GROUP])
            def _(row=row, src=src, dst=dst):
                dst[here, :] = src[slot(order, row, k), :]

            @pl.when(k >= order[row, GROUP])
            def _(dst=dst):
                dst[here, :] = jnp.zeros((DT, FT), BF)

        @pl.when(k < order[0, GROUP])
        def _():
            pd[:, here] = dw[:, slot(order, 0, k)]

        @pl.when(k >= order[0, GROUP])
        def _():
            pd[:, here] = jnp.zeros((FT, DT), BF)


def cot_pack_body(order, *refs):
    pieces, outs = refs[:NZ], refs[NZ:]
    for dx in range(NX):
        for k in range(KMAX):
            where = slot(order, dx, k)
            for dz in range(NZ):
                outs[dx][dz * 16:(dz + 1) * 16, k * DT:(k + 1) * DT] = pieces[dz][:, where]


def gate_up_body(order, meta, *refs):
    pieces = refs[:NZ]
    pg, pu, tg, tu, keep, send = refs[NZ:]
    for row, dst in ((4, tg), (5, tu)):
        for k in range(KMAX):
            where = slot(order, row, k)
            for dz in range(NZ):
                for dx in range(NX):
                    dst[dx * 128 + dz * 16:dx * 128 + dz * 16 + 16, k * DT:(k + 1) * DT] = (
                        pieces[dz][dx * 16:(dx + 1) * 16, where]
                    )
    c = meta[4]
    mine = pl.ds(pl.multiple_of(c * 256, 256), 256)
    other = pl.ds(pl.multiple_of((1 - c) * 256, 256), 256)
    for i, (src, w) in enumerate(((tg, pg), (tu, pu))):
        send[i] = jnp.dot(src[other, :], w[...], preferred_element_type=F32)
    for i, (src, w) in enumerate(((tg, pg), (tu, pu))):
        keep[i] = jnp.dot(src[mine, :], w[...], preferred_element_type=F32)


def nt(a, b):
    return lax.dot_general(a, b, (((1,), (1,)), ((), ())), preferred_element_type=F32)


def back_body(meta, c0, c1, c2, c3, pd, keep, send):
    c = meta[4]

    @pl.when(c == 0)
    def _():
        send[0:128, :] = nt(c2[...], pd[...])
        send[128:256, :] = nt(c3[...], pd[...])
        keep[0:128, :] = nt(c0[...], pd[...])
        keep[128:256, :] = nt(c1[...], pd[...])

    @pl.when(c == 1)
    def _():
        send[0:128, :] = nt(c0[...], pd[...])
        send[128:256, :] = nt(c1[...], pd[...])
        keep[0:128, :] = nt(c2[...], pd[...])
        keep[128:256, :] = nt(c3[...], pd[...])


def join(meta, a, b, full):
    c = meta[4]
    full[pl.ds(pl.multiple_of(c * 256, 256), 256), :] = a
    full[pl.ds(pl.multiple_of((1 - c) * 256, 256), 256), :] = b


def act_body(own, got, hid, silu_out, slope_out):
    g = own[0] + got[0].astype(F32)
    u = own[1] + got[1].astype(F32)
    s = jax.nn.sigmoid(g)
    silu = g * s
    hid[...] = (silu * u).astype(BF)
    silu_out[...] = silu
    slope_out[...] = u * s * (1.0 + g * (1.0 - s))


def act_back_body(own, got, silu, slope, acts):
    b = own[...] + got[...].astype(F32)
    acts[0] = (b * slope[...]).astype(BF)
    acts[1] = (b * silu[...]).astype(BF)


def out_body(meta, ha, hb, pd, o0, o1, o2, o3, full):
    join(meta, ha[...], hb[...], full)
    for dx, o in ((2, o2), (1, o1), (3, o3), (0, o0)):
        o[...] = jnp.dot(full[dx * 128:(dx + 1) * 128, :], pd[...], preferred_element_type=F32).astype(o.dtype)


def out_sum_body(order, p0, p1, p2, p3, *refs):
    outs, acc = refs[:NZ], refs[NZ]
    acc[...] = jnp.zeros_like(acc)
    for dx, p in enumerate((p0, p1, p2, p3)):
        for k in range(KMAX):
            where = slot(order, dx, k)
            acc[:, where] = acc[:, where] + p[:, k * DT:(k + 1) * DT].astype(F32)
    for dz in range(NZ):
        outs[dz][...] = acc[dz * 16:(dz + 1) * 16, :].astype(outs[dz].dtype)


def tok_grad_body(order, meta, aa, ab, pg, pu, *refs):
    outs, gfull, ufull, acc = refs[:NZ], refs[NZ], refs[NZ + 1], refs[NZ + 2]
    join(meta, aa[0], ab[0], gfull)
    join(meta, aa[1], ab[1], ufull)
    acc[...] = jnp.zeros_like(acc)
    for row, act, w in ((4, gfull, pg), (5, ufull, pu)):
        for k in range(0, KMAX, 2):
            r = nt(act[...], w[k * DT:(k + 2) * DT, :])
            for i in range(2):
                where = slot(order, row, k + i)
                acc[:, where] = acc[:, where] + r[:, i * DT:(i + 1) * DT]
    for dz in range(NZ):
        for dx in range(NX):
            outs[dz][dx * 16:(dx + 1) * 16, :] = acc[dx * 128 + dz * 16:dx * 128 + dz * 16 + 16, :].astype(outs[dz].dtype)


def weight_grad_body(order, meta, aa, ab, tg, tu, gg, gu, gfull, ufull):
    join(meta, aa[0], ab[0], gfull)
    join(meta, aa[1], ab[1], ufull)
    for row, act, tok, dst in ((4, gfull, tg, gg), (5, ufull, tu, gu)):
        dst[...] = jnp.zeros_like(dst)
        for k in range(KMAX):
            @pl.when(k < order[row, GROUP])
            def _(row=row, act=act, tok=tok, dst=dst, k=k):
                dst[slot(order, row, k), :] = jnp.dot(
                    tok[:, k * DT:(k + 1) * DT].T, act[...], preferred_element_type=F32
                ).astype(BF)


def down_grad_body(order, meta, ha, hb, c0, c1, c2, c3, gd, full, flip, cp):
    join(meta, ha[...], hb[...], full)
    flip[...] = full[...].T
    for dx, c in enumerate((c0, c1, c2, c3)):
        cp[dx * 128:(dx + 1) * 128, :] = c[...]
    gd[...] = jnp.zeros_like(gd)
    for k in range(KMAX):
        @pl.when(k < order[0, GROUP])
        def _(k=k):
            gd[:, slot(order, 0, k)] = jnp.dot(
                flip[...], cp[:, k * DT:(k + 1) * DT], preferred_element_type=F32
            ).astype(BF)


def ring_gather(v):
    up, down = [v], [v]
    for k in range(4):
        up.append(shift(up[-1], dz=1))
        if k < 3:
            down.append(shift(down[-1], dz=-1))
    return up + down[:0:-1]


def ring_scatter(p, wire):
    lo, hi = p[4], p[5]
    for k in range(4):
        lo = shift(lo.astype(wire), dz=-1)
        if k < 3:
            hi = shift(hi.astype(wire), dz=1)
        if k < 3:
            lo = lo.astype(F32) + p[3 - k]
        if k < 2:
            hi = hi.astype(F32) + p[6 + k]
    return p[0] + lo.astype(F32) + hi.astype(F32)


def local(tokens, gate_weight, up_weight, down_weight, gate_mask, up_mask, down_mask, cotangent):
    f = lax.axis_index("fsdp")
    t = lax.axis_index("tensor")
    meta = jnp.stack([f // (NX * NY), f // NY % NX, f % NY, t, t % 2]).astype(jnp.int32)

    both = jnp.concatenate([tokens, cotangent], axis=0)
    near = shift(both, dy=1)
    tok = jnp.concatenate([tokens, near[:8]], axis=0)
    cot = jnp.concatenate([cotangent, near[8:]], axis=0)

    mflop = 2 * T * PK * FT
    order, pg, pu, pd = call(
        prep_body,
        (sds((6, GROUP + 1), jnp.int32), sds((PK, FT), BF), sds((PK, FT), BF), sds((FT, PK), BF)),
        [SMEM] * 4 + [VMEM] * 3,
        (SMEM, VMEM, VMEM, VMEM),
        moved=9000000,
    )(meta, gate_mask, up_mask, down_mask, gate_weight, up_weight, down_weight)

    tok64 = jnp.concatenate([tok] + [shift(tok, dx=d) for d in (1, 2, 3)], axis=0)
    tok_pieces = ring_gather(tok64)

    cot_pieces = ring_gather(cot)
    cots = call(
        cot_pack_body,
        tuple(sds((128, PK), BF) for _ in range(NX)),
        [SMEM] + [VMEM] * NZ,
        (VMEM,) * NX,
        moved=2000000,
    )(order, *cot_pieces)
    cots = [cots[0]] + [shift(cots[d], dx=d) for d in (1, 2, 3)]

    half = sds((2, 256, FT), F32)
    tg, tu, keep, send = call(
        gate_up_body,
        (sds((T, PK), BF), sds((T, PK), BF), half, half),
        [SMEM] * 2 + [VMEM] * (NZ + 2),
        (VMEM,) * 4,
        flops=2 * mflop, moved=8000000,
    )(order, meta, *tok_pieces, pg, pu)
    sums = keep + swap_core(send)
    far = swap_far(sums.astype(BF))
    hid, silu, slope = call(
        act_body,
        (sds((256, FT), BF), sds((256, FT), F32), sds((256, FT), F32)),
        [VMEM] * 2,
        (VMEM,) * 3,
        moved=3000000,
    )(sums, far)
    hid_other = swap_core(hid)

    bkeep, bsend = call(
        back_body,
        (sds((256, FT), F32), sds((256, FT), F32)),
        [SMEM] + [VMEM] * 5,
        (VMEM,) * 2,
        flops=mflop, moved=3000000,
    )(meta, *cots, pd)
    bsums = bkeep + swap_core(bsend)
    bfar = swap_far(bsums.astype(BF))
    acts = call(
        act_back_body, sds((2, 256, FT), BF), [VMEM] * 4, VMEM, moved=2000000
    )(bsums, bfar, silu, slope)
    acts_other = swap_core(acts)

    outs = call(
        out_body,
        (sds((128, PK), F32),) + (sds((128, PK), BF),) * 3,
        [SMEM] + [VMEM] * 3,
        (VMEM,) * 4,
        [pltpu.VMEM((T, FT), BF)],
        flops=mflop, moved=2000000,
    )(meta, hid, hid_other, pd)
    outs = [outs[0]] + [shift(outs[d], dx=-d) for d in (1, 2, 3)]
    first = (4, 5)
    parts = call(
        out_sum_body,
        tuple(sds((16, W), BF if dz in first else F32) for dz in range(NZ)),
        [SMEM] + [VMEM] * 4,
        (VMEM,) * NZ,
        [pltpu.VMEM((128, W), F32)],
        moved=3000000,
    )(order, *outs)
    mine = ring_scatter(parts, BF)
    ffn_output = (mine[:8] + shift(mine[8:], dy=1)).astype(BF)

    parts = call(
        tok_grad_body,
        tuple(sds((64, W), BF if dz in first else F32) for dz in range(NZ)),
        [SMEM] * 2 + [VMEM] * 4,
        (VMEM,) * NZ,
        [pltpu.VMEM((T, FT), BF), pltpu.VMEM((T, FT), BF), pltpu.VMEM((T, W), F32)],
        flops=2 * mflop, moved=8000000,
    )(order, meta, acts, acts_other, pg, pu)
    mine = ring_scatter(parts, BF)
    mine = mine[:16] + sum(shift(mine[16 * d:16 * d + 16], dx=-d) for d in (1, 2, 3))
    grad_tokens = (mine[:8] + shift(mine[8:], dy=1)).astype(BF)

    grad_down = call(
        down_grad_body,
        sds((FT, W), BF),
        [SMEM] * 2 + [VMEM] * 6,
        VMEM,
        [pltpu.VMEM((T, FT), BF), pltpu.VMEM((FT, T), BF), pltpu.VMEM((T, PK), BF)],
        flops=mflop, moved=5000000,
    )(order, meta, hid, hid_other, *cots)
    grad_gate, grad_up = call(
        weight_grad_body,
        (sds((W, FT), BF), sds((W, FT), BF)),
        [SMEM] * 2 + [VMEM] * 4,
        (VMEM,) * 2,
        [pltpu.VMEM((T, FT), BF), pltpu.VMEM((T, FT), BF)],
        flops=2 * mflop, moved=9000000,
    )(order, meta, acts, acts_other, tg, tu)
    return (ffn_output, grad_tokens, grad_gate, grad_up, grad_down)


def solution(mesh):
    return jax.shard_map(
        local,
        mesh=mesh,
        in_specs=(
            P("fsdp", "tensor"),
            P("tensor", "fsdp"),
            P("tensor", "fsdp"),
            P("fsdp", "tensor"),
            P(),
            P(),
            P(),
            P("fsdp", "tensor"),
        ),
        out_specs=(
            P("fsdp", "tensor"),
            P("fsdp", "tensor"),
            P("tensor", "fsdp"),
            P("tensor", "fsdp"),
            P("fsdp", "tensor"),
        ),
        check_vma=False,
    )
```

```python
import functools
import jax
import jax.numpy as jnp
from jax import lax
from jax.experimental import pallas as pl
from jax.experimental.pallas import tpu as pltpu
from jax.sharding import PartitionSpec as P

NZ, NX, NY = 8, 4, 2
NBLK, GROUP, KMAX = 64, 16, 8
DT, FT = 128, 448
W = GROUP * DT
PK = KMAX * DT
T = 512
BF, F32 = jnp.bfloat16, jnp.float32
VMEM = pl.BlockSpec(memory_space=pltpu.VMEM)
SMEM = pl.BlockSpec(memory_space=pltpu.SMEM)


def fsdp_perm(dz, dx, dy):
    pairs = []
    for z in range(NZ):
        for x in range(NX):
            for y in range(NY):
                src = (z * NX + x) * NY + y
                dst = ((z + dz) % NZ * NX + (x + dx) % NX) * NY + (y + dy) % NY
                pairs.append((src, dst))
    return pairs


def shift(v, dz=0, dx=0, dy=0):
    return lax.ppermute(v, "fsdp", fsdp_perm(dz, dx, dy))


def swap_core(v):
    return lax.ppermute(v, "tensor", [(i, i ^ 1) for i in range(4)])


def swap_far(v):
    return lax.ppermute(v, "tensor", [(i, i ^ 2) for i in range(4)])


def call(body, outs, in_specs, out_specs, scratch=(), mib=20):
    return pl.pallas_call(
        body,
        out_shape=outs,
        in_specs=in_specs,
        out_specs=out_specs,
        scratch_shapes=list(scratch),
        compiler_params=pltpu.CompilerParams(vmem_limit_bytes=mib * 1024 * 1024),
        cost_estimate=pl.CostEstimate(flops=1, bytes_accessed=1, transcendentals=0),
    )


def sds(shape, dtype):
    return jax.ShapeDtypeStruct(shape, dtype)


def slot(order, row, k):
    return pl.ds(pl.multiple_of(order[row, k] * DT, DT), DT)


def order_body(meta, gm_in, um_in, dm_in, order, gm, um, dm, sem):
    loads = [
        pltpu.make_async_copy(src, dst, sem.at[i])
        for i, (src, dst) in enumerate(((gm_in, gm), (um_in, um), (dm_in, dm)))
    ]
    for load in loads:
        load.start()
    for load in loads:
        load.wait()
    z, x, y, t = meta[0], meta[1], meta[2], meta[3]
    for row in range(6):
        fx = lax.rem(x + row, NX) if row < 4 else x
        f = (z * NX + fx) * NY + y
        for k in range(KMAX + 1):
            order[row, k] = 0
        n = jnp.int32(0)
        for j in range(GROUP):
            if row < 4:
                m = dm[f, t * GROUP + j]
            elif row == 4:
                m = gm[t * GROUP + j, f]
            else:
                m = um[t * GROUP + j, f]
            order[row, n] = j
            n = n + m
        order[row, GROUP] = n


def live(order, row, k, v):
    return jnp.where(k < order[row, GROUP], v, jnp.zeros_like(v))


def pair(order, row, k, ref):
    return jnp.concatenate([ref[:, slot(order, row, k)], ref[:, slot(order, row, k + 1)]], axis=1)


COT_ROW = (0, 0, 32, 32, 32, 32, 32, 0)


def cot_pack_body(order, *refs):
    pieces, outs = refs[:NZ], refs[NZ:]
    for dx in range(NX):
        for k in range(KMAX):
            where = slot(order, dx, k)
            for dz in range(NZ):
                outs[dx][dz * 16:(dz + 1) * 16, k * DT:(k + 1) * DT] = live(
                    order, dx, k, pieces[dz][COT_ROW[dz]:COT_ROW[dz] + 16, where]
                )


def nt(a, b):
    return lax.dot_general(a, b, (((1,), (1,)), ((), ())), preferred_element_type=F32)


def gate_up_body(order, meta, *refs):
    pieces = refs[:NZ], refs[NZ:2 * NZ]
    gw, uw, tg, tu, keep, send = refs[2 * NZ:]
    for row, dst in ((4, tg), (5, tu)):
        for k in range(KMAX):
            where = slot(order, row, k)
            for dz in range(NZ):
                for dx in range(NX):
                    dst[dx * 128 + dz * 16:dx * 128 + dz * 16 + 16, k * DT:(k + 1) * DT] = live(
                        order, row, k, pieces[dx // 2][dz][dx % 2 * 16:(dx % 2 + 1) * 16, where]
                    )
    c = meta[4]
    mine = pl.ds(pl.multiple_of(c * 256, 256), 256)
    other = pl.ds(pl.multiple_of((1 - c) * 256, 256), 256)
    for rows, dst in ((other, send), (mine, keep)):
        for here, row, w, tok in ((slice(0, FT), 4, gw, tg), (slice(FT, 2 * FT), 5, uw, tu)):
            dst[here, :] = sum(
                nt(pair(order, row, k, w), tok[rows, k * DT:(k + 2) * DT]) for k in range(0, KMAX, 2)
            )


def back_body(order, meta, c0, c1, c2, c3, dw, keep, send):
    def fill(dst, a, b):
        for i, c in ((0, a), (128, b)):
            dst[:, i:i + 128] = sum(
                nt(pair(order, 0, k, dw), c[:, k * DT:(k + 2) * DT]) for k in range(0, KMAX, 2)
            )

    @pl.when(meta[4] == 0)
    def _():
        fill(send, c2, c3)
        fill(keep, c0, c1)

    @pl.when(meta[4] == 1)
    def _():
        fill(send, c0, c1)
        fill(keep, c2, c3)


def join(meta, a, b, full):
    c = meta[4]
    full[:, pl.ds(pl.multiple_of(c * 256, 256), 256)] = a
    full[:, pl.ds(pl.multiple_of((1 - c) * 256, 256), 256)] = b


def act_body(own, bown, got, bgot, acts):
    g = own[:FT, :] + got[:FT, :].astype(F32)
    u = own[FT:, :] + got[FT:, :].astype(F32)
    b = bown[...] + bgot[...].astype(F32)
    s = jax.nn.sigmoid(g)
    silu = g * s
    acts[:FT, :] = (silu * u).astype(BF)
    acts[FT:2 * FT, :] = (b * u * s * (1.0 + g * (1.0 - s))).astype(BF)
    acts[2 * FT:, :] = (b * silu).astype(BF)


def out_body(order, meta, aa, ab, dw, o0, o1, o2, o3, full, flip):
    join(meta, aa[:FT, :], ab[:FT, :], full)
    flip[...] = full[...].T
    for dx, o in ((2, o2), (1, o1), (3, o3), (0, o0)):
        for k in range(0, KMAX, 2):
            r = jnp.dot(flip[dx * 128:(dx + 1) * 128, :], pair(order, 0, k, dw), preferred_element_type=F32)
            for i in range(2):
                o[:, (k + i) * DT:(k + i + 1) * DT] = live(order, 0, k + i, r[:, i * DT:(i + 1) * DT]).astype(o.dtype)


def tok_grad_body(order, meta, aa, ab, gw, uw, near, *refs):
    outs = refs[:NZ]
    full, gflip, uflip, acc = refs[NZ:]
    join(meta, aa[FT:2 * FT, :], ab[FT:2 * FT, :], full)
    gflip[...] = full[...].T
    join(meta, aa[2 * FT:, :], ab[2 * FT:, :], full)
    uflip[...] = full[...].T
    for half, dst in ((1, acc), (0, near)):
        rows = slice(half * 256, half * 256 + 256)
        dst[...] = jnp.zeros_like(dst)
        for row, act, w in ((4, gflip, gw), (5, uflip, uw)):
            for k in range(0, KMAX, 2):
                r = jnp.dot(act[rows, :], pair(order, row, k, w), preferred_element_type=F32)
                for i in range(2):
                    where = slot(order, row, k + i)
                    dst[:, where] = dst[:, where] + live(order, row, k + i, r[:, i * DT:(i + 1) * DT])
    for dz in range(NZ):
        o = outs[dz]
        for i in range(2):
            o[i * 16:(i + 1) * 16, :] = acc[i * 128 + dz * 16:i * 128 + dz * 16 + 16, :].astype(o.dtype)


def merge_body(order, p0, p1, p2, p3, near, *refs):
    outs, acc = refs[:NZ], refs[NZ]
    acc[...] = jnp.zeros_like(acc)
    for dx, p in enumerate((p0, p1, p2, p3)):
        for k in range(KMAX):
            where = slot(order, dx, k)
            acc[:, where] = acc[:, where] + p[:, k * DT:(k + 1) * DT].astype(F32)
    for dz in range(NZ):
        o = outs[dz]
        for i in range(2):
            o[i * 16:(i + 1) * 16, :] = near[i * 128 + dz * 16:i * 128 + dz * 16 + 16, :].astype(o.dtype)
        o[32:48, :] = acc[dz * 16:(dz + 1) * 16, :].astype(o.dtype)


def scatter_blocks(order, row, act, packed, dst):
    dst[...] = jnp.zeros_like(dst)
    for k in range(0, KMAX, 2):
        @pl.when(k < order[row, GROUP])
        def _(k=k):
            r = jnp.dot(act[...], packed[:, k * DT:(k + 2) * DT], preferred_element_type=F32).astype(BF)
            dst[:, slot(order, row, k)] = r[:, :DT]

            @pl.when(k + 1 < order[row, GROUP])
            def _():
                dst[:, slot(order, row, k + 1)] = r[:, DT:]


def weight_grad_body(row, order, meta, aa, ab, tok, dst, full):
    here = slice((row - 3) * FT, (row - 2) * FT)
    join(meta, aa[here, :], ab[here, :], full)
    scatter_blocks(order, row, full, tok, dst)


def down_grad_body(order, meta, aa, ab, c0, c1, c2, c3, gd, full, cp):
    join(meta, aa[:FT, :], ab[:FT, :], full)
    for dx, c in enumerate((c0, c1, c2, c3)):
        cp[dx * 128:(dx + 1) * 128, :] = c[...]
    scatter_blocks(order, 0, full, cp, gd)


def sync(*values):
    return lax.optimization_barrier(values)


def ring_gather(v):
    up, down = [v], [v]
    for k in range(4):
        up.append(shift(up[-1], dz=1))
        if k < 3:
            down.append(shift(down[-1], dz=-1))
    return up + down[:0:-1]


class Scatter:
    def __init__(self, p):
        self.p, self.k = p, 0
        self.lo, self.hi = p[4], p[5]

    def step(self):
        k, p = self.k, self.p
        lo = shift(self.lo, dz=-1)
        hi = shift(self.hi, dz=1) if k < 3 else None
        self.k = k + 1
        if k < 3:
            self.lo = (lo.astype(F32) + p[3 - k]).astype(BF)
            self.hi = (hi.astype(F32) + p[6 + k]).astype(BF) if k < 2 else hi
            return
        self.total = p[0] + lo.astype(F32) + self.hi.astype(F32)

    def after(self, value):
        self.lo, value = sync(self.lo, value)
        return value


def local(tokens, gate_weight, up_weight, down_weight, gate_mask, up_mask, down_mask, cotangent):
    f = lax.axis_index("fsdp")
    t = lax.axis_index("tensor")
    meta = jnp.stack([f // (NX * NY), f // NY % NX, f % NY, t, t % 2]).astype(jnp.int32)

    near = shift(jnp.concatenate([tokens, cotangent], axis=0), dy=1)
    hbm = pl.BlockSpec(memory_space=pltpu.HBM)
    order = call(
        order_body,
        sds((6, GROUP + 1), jnp.int32),
        [SMEM] + [hbm] * 3,
        SMEM,
        [pltpu.SMEM((NBLK, NBLK), jnp.int32)] * 3 + [pltpu.SemaphoreType.DMA((3,))],
        mib=60,
    )(meta, gate_mask, up_mask, down_mask)
    near, order = sync(near, jnp.maximum(order, 0))
    gate_weight, up_weight = gate_weight.T, up_weight.T
    tok = jnp.concatenate([tokens, near[:8]], axis=0)
    cot = jnp.concatenate([cotangent, near[8:]], axis=0)

    wide = [tok] + [shift(tok, dx=d) for d in (1, 2, 3)]
    cot_up, cot_down = shift(cot, dz=1), shift(cot, dz=-1)
    tok_a = jnp.concatenate(wide[:2], axis=0)
    up = [shift(jnp.concatenate([tok_a, cot_up], axis=0), dz=1)]
    down = [shift(jnp.concatenate([tok_a, cot_down], axis=0), dz=-1)]
    up.append(shift(up[-1], dz=1))
    down.append(shift(down[-1], dz=-1))
    up.append(shift(up[-1], dz=1))
    down.append(shift(down[-1][:32], dz=-1))
    up.append(shift(up[-1][:32], dz=1))
    pieces_b = ring_gather(jnp.concatenate(wide[2:], axis=0))
    cots = call(
        cot_pack_body,
        tuple(sds((128, PK), BF) for _ in range(NX)),
        [SMEM] + [VMEM] * NZ,
        (VMEM,) * NX,
    )(order, cot, cot_up, up[0], up[1], up[2], down[1], down[0], cot_down)
    pieces_a = [tok_a] + up + down[::-1]
    pieces_a, pieces_b, cots = sync(pieces_a, pieces_b, cots)
    tg, tu, keep, send = call(
        gate_up_body,
        (sds((T, PK), BF), sds((T, PK), BF), sds((2 * FT, 256), F32), sds((2 * FT, 256), F32)),
        [SMEM] * 2 + [VMEM] * (2 * NZ + 2),
        (VMEM,) * 4,
    )(order, meta, *pieces_a, *pieces_b, gate_weight, up_weight)
    cots = [cots[0]] + [shift(cots[d], dx=d) for d in (1, 2, 3)]
    cots, keep, send = sync(cots, keep, send)
    sums = keep + swap_core(send)
    far = swap_far(sums.astype(BF))
    bkeep, bsend = call(
        back_body,
        (sds((FT, 256), F32), sds((FT, 256), F32)),
        [SMEM] * 2 + [VMEM] * 5,
        (VMEM,) * 2,
    )(order, meta, *cots, down_weight)
    bsums = bkeep + swap_core(bsend)
    bfar = swap_far(bsums.astype(BF))
    far, bfar = sync(far, bfar)
    acts = call(act_body, sds((3 * FT, 256), BF), [VMEM] * 4, VMEM)(sums, bsums, far, bfar)
    acts_other = swap_core(acts)
    outs = call(
        out_body,
        (sds((128, PK), F32),) + (sds((128, PK), BF),) * 3,
        [SMEM] * 2 + [VMEM] * 3,
        (VMEM,) * 4,
        [pltpu.VMEM((FT, T), BF), pltpu.VMEM((T, FT), BF)],
    )(order, meta, acts, acts_other, down_weight)
    acts, *outs = sync(acts, *outs)
    outs = [outs[0]] + [shift(outs[d], dx=-d) for d in (1, 2, 3)]
    first = (4, 5)
    near, *parts_b = call(
        tok_grad_body,
        (sds((256, W), F32),) + tuple(sds((32, W), BF if dz in first else F32) for dz in range(NZ)),
        [SMEM] * 2 + [VMEM] * 4,
        (VMEM,) * (NZ + 1),
        [pltpu.VMEM((FT, T), BF), pltpu.VMEM((T, FT), BF), pltpu.VMEM((T, FT), BF), pltpu.VMEM((256, W), F32)],
    )(order, meta, acts, acts_other, gate_weight, up_weight)
    near, outs = sync(near, outs)
    parts_a = call(
        merge_body,
        tuple(sds((48, W), BF if dz in first else F32) for dz in range(NZ)),
        [SMEM] + [VMEM] * 5,
        (VMEM,) * NZ,
        [pltpu.VMEM((128, W), F32)],
    )(order, *outs, near)

    full = pltpu.VMEM((FT, T), BF)

    def down_grad(cots):
        return call(
            down_grad_body,
            sds((FT, W), BF),
            [SMEM] * 2 + [VMEM] * 6,
            VMEM,
            [full, pltpu.VMEM((T, PK), BF)],
        )(order, meta, acts, acts_other, *cots)

    def weight_grad(row, tok):
        return call(
            functools.partial(weight_grad_body, row),
            sds((FT, W), BF),
            [SMEM] * 2 + [VMEM] * 3,
            VMEM,
            [full],
        )(order, meta, acts, acts_other, tok)

    ring_a, ring_b = Scatter(list(parts_a)), Scatter(list(parts_b))
    ring_b.step()
    cots = ring_b.after(cots)
    grad_down = down_grad(cots)
    ring_a.step()
    tg, grad_down = ring_a.after((tg, grad_down))
    grad_gate = weight_grad(4, tg)
    ring_b.step()
    ring_a.step()
    tu, grad_gate = ring_a.after((tu, grad_gate))
    grad_up = weight_grad(5, tu)
    ring_b.step()
    ring_a.step()
    grad_up = ring_a.after(grad_up)
    ring_b.step()
    ring_a.step()
    a, b = ring_a.total, ring_b.total
    mine = a[:16]
    for d, far in ((1, a[16:32]), (2, b[:16]), (3, b[16:])):
        mine = mine + shift(far.astype(BF), dx=-d).astype(F32)
    out = a[32:]
    grad_tokens = (mine[:8] + shift(mine[8:], dy=1)).astype(BF)
    ffn_output = (out[:8] + shift(out[8:], dy=1)).astype(BF)
    return (ffn_output, grad_tokens, grad_gate.T, grad_up.T, grad_down)


def solution(mesh):
    return jax.shard_map(
        local,
        mesh=mesh,
        in_specs=(
            P("fsdp", "tensor"),
            P("tensor", "fsdp"),
            P("tensor", "fsdp"),
            P("fsdp", "tensor"),
            P(),
            P(),
            P(),
            P("fsdp", "tensor"),
        ),
        out_specs=(
            P("fsdp", "tensor"),
            P("fsdp", "tensor"),
            P("tensor", "fsdp"),
            P("tensor", "fsdp"),
            P("fsdp", "tensor"),
        ),
        check_vma=False,
    )
```

```python
import functools
import jax
import jax.numpy as jnp
from jax import lax
from jax.experimental import pallas as pl
from jax.experimental.pallas import tpu as pltpu
from jax.sharding import PartitionSpec as P

NZ, NX, NY = 8, 4, 2
NBLK, GROUP, KMAX = 64, 16, 8
DT, FT = 128, 448
W = GROUP * DT
PK = KMAX * DT
T = 512
BF, F32 = jnp.bfloat16, jnp.float32
VMEM = pl.BlockSpec(memory_space=pltpu.VMEM)
SMEM = pl.BlockSpec(memory_space=pltpu.SMEM)


def fsdp_perm(dz, dx, dy):
    pairs = []
    for z in range(NZ):
        for x in range(NX):
            for y in range(NY):
                src = (z * NX + x) * NY + y
                dst = ((z + dz) % NZ * NX + (x + dx) % NX) * NY + (y + dy) % NY
                pairs.append((src, dst))
    return pairs


def shift(v, dz=0, dx=0, dy=0):
    return lax.ppermute(v, "fsdp", fsdp_perm(dz, dx, dy))


def swap_core(v):
    return lax.ppermute(v, "tensor", [(i, i ^ 1) for i in range(4)])


def swap_far(v):
    return lax.ppermute(v, "tensor", [(i, i ^ 2) for i in range(4)])


def call(body, outs, in_specs, out_specs, scratch=(), mib=20):
    return pl.pallas_call(
        body,
        out_shape=outs,
        in_specs=in_specs,
        out_specs=out_specs,
        scratch_shapes=list(scratch),
        compiler_params=pltpu.CompilerParams(vmem_limit_bytes=mib * 1024 * 1024),
        cost_estimate=pl.CostEstimate(flops=1, bytes_accessed=1, transcendentals=0),
    )


def sds(shape, dtype):
    return jax.ShapeDtypeStruct(shape, dtype)


def slot(order, row, k):
    return pl.ds(pl.multiple_of(order[row, k] * DT, DT), DT)


def order_body(meta, gm_in, um_in, dm_in, order, gm, um, dm, sem):
    loads = [
        pltpu.make_async_copy(src, dst, sem.at[i])
        for i, (src, dst) in enumerate(((gm_in, gm), (um_in, um), (dm_in, dm)))
    ]
    for load in loads:
        load.start()
    for load in loads:
        load.wait()
    z, x, y, t = meta[0], meta[1], meta[2], meta[3]
    for row in range(6):
        fx = lax.rem(x + row, NX) if row < 4 else x
        f = (z * NX + fx) * NY + y
        for k in range(KMAX + 1):
            order[row, k] = 0
        n = jnp.int32(0)
        for j in range(GROUP):
            if row < 4:
                m = dm[f, t * GROUP + j]
            elif row == 4:
                m = gm[t * GROUP + j, f]
            else:
                m = um[t * GROUP + j, f]
            order[row, n] = j
            n = n + m
        order[row, GROUP] = n


def live(order, row, k, v):
    return jnp.where(k < order[row, GROUP], v, jnp.zeros_like(v))


def pair(order, row, k, ref):
    return jnp.concatenate([ref[:, slot(order, row, k)], ref[:, slot(order, row, k + 1)]], axis=1)


COT_ROW = (0, 0, 32, 32, 32, 32, 32, 0)


def cot_pack_body(order, *refs):
    pieces, outs = refs[:NZ], refs[NZ:]
    for dx in range(NX):
        for k in range(KMAX):
            where = slot(order, dx, k)
            for dz in range(NZ):
                outs[dx][dz * 16:(dz + 1) * 16, k * DT:(k + 1) * DT] = live(
                    order, dx, k, pieces[dz][COT_ROW[dz]:COT_ROW[dz] + 16, where]
                )


def nt(a, b):
    return lax.dot_general(a, b, (((1,), (1,)), ((), ())), preferred_element_type=F32)


def gate_up_body(order, meta, *refs):
    pieces = refs[:NZ], refs[NZ:2 * NZ]
    gw, uw, tg, tu, keep, send = refs[2 * NZ:]
    for row, dst in ((4, tg), (5, tu)):
        for k in range(KMAX):
            where = slot(order, row, k)
            for dz in range(NZ):
                for dx in range(NX):
                    dst[dx * 128 + dz * 16:dx * 128 + dz * 16 + 16, k * DT:(k + 1) * DT] = live(
                        order, row, k, pieces[dx // 2][dz][dx % 2 * 16:(dx % 2 + 1) * 16, where]
                    )
    c = meta[4]
    mine = pl.ds(pl.multiple_of(c * 256, 256), 256)
    other = pl.ds(pl.multiple_of((1 - c) * 256, 256), 256)
    for rows, dst in ((other, send), (mine, keep)):
        for here, row, w, tok in ((slice(0, FT), 4, gw, tg), (slice(FT, 2 * FT), 5, uw, tu)):
            dst[here, :] = sum(
                nt(pair(order, row, k, w), tok[rows, k * DT:(k + 2) * DT]) for k in range(0, KMAX, 2)
            )


def back_body(order, meta, c0, c1, c2, c3, dw, keep, send):
    def fill(dst, a, b):
        for i, c in ((0, a), (128, b)):
            dst[:, i:i + 128] = sum(
                nt(pair(order, 0, k, dw), c[:, k * DT:(k + 2) * DT]) for k in range(0, KMAX, 2)
            )

    @pl.when(meta[4] == 0)
    def _():
        fill(send, c2, c3)
        fill(keep, c0, c1)

    @pl.when(meta[4] == 1)
    def _():
        fill(send, c0, c1)
        fill(keep, c2, c3)


def join(meta, a, b, full):
    c = meta[4]
    full[:, pl.ds(pl.multiple_of(c * 256, 256), 256)] = a
    full[:, pl.ds(pl.multiple_of((1 - c) * 256, 256), 256)] = b


def act_body(own, bown, got, bgot, acts):
    g = own[:FT, :] + got[:FT, :].astype(F32)
    u = own[FT:, :] + got[FT:, :].astype(F32)
    b = bown[...] + bgot[...].astype(F32)
    s = jax.nn.sigmoid(g)
    silu = g * s
    acts[:FT, :] = (silu * u).astype(BF)
    acts[FT:2 * FT, :] = (b * u * s * (1.0 + g * (1.0 - s))).astype(BF)
    acts[2 * FT:, :] = (b * silu).astype(BF)


def out_body(order, meta, aa, ab, dw, o0, o1, o2, o3, full, flip):
    join(meta, aa[:FT, :], ab[:FT, :], full)
    flip[...] = full[...].T
    for dx, o in ((2, o2), (1, o1), (3, o3), (0, o0)):
        for k in range(0, KMAX, 2):
            r = jnp.dot(flip[dx * 128:(dx + 1) * 128, :], pair(order, 0, k, dw), preferred_element_type=F32)
            for i in range(2):
                o[:, (k + i) * DT:(k + i + 1) * DT] = live(order, 0, k + i, r[:, i * DT:(i + 1) * DT]).astype(o.dtype)


def tok_grad_body(order, meta, aa, ab, gw, uw, near, *refs):
    outs = refs[:NZ]
    full, gflip, uflip, acc = refs[NZ:]
    join(meta, aa[FT:2 * FT, :], ab[FT:2 * FT, :], full)
    gflip[...] = full[...].T
    join(meta, aa[2 * FT:, :], ab[2 * FT:, :], full)
    uflip[...] = full[...].T
    for half, dst in ((1, acc), (0, near)):
        rows = slice(half * 256, half * 256 + 256)
        dst[...] = jnp.zeros_like(dst)
        for row, act, w in ((4, gflip, gw), (5, uflip, uw)):
            for k in range(0, KMAX, 2):
                r = jnp.dot(act[rows, :], pair(order, row, k, w), preferred_element_type=F32)
                for i in range(2):
                    where = slot(order, row, k + i)
                    dst[:, where] = dst[:, where] + live(order, row, k + i, r[:, i * DT:(i + 1) * DT])
    for dz in range(NZ):
        o = outs[dz]
        for i in range(2):
            o[i * 16:(i + 1) * 16, :] = acc[i * 128 + dz * 16:i * 128 + dz * 16 + 16, :].astype(o.dtype)


def merge_body(order, p0, p1, p2, p3, near, *refs):
    outs, acc = refs[:NZ], refs[NZ]
    acc[...] = jnp.zeros_like(acc)
    for dx, p in enumerate((p0, p1, p2, p3)):
        for k in range(KMAX):
            where = slot(order, dx, k)
            acc[:, where] = acc[:, where] + p[:, k * DT:(k + 1) * DT].astype(F32)
    for dz in range(NZ):
        o = outs[dz]
        for i in range(2):
            o[i * 16:(i + 1) * 16, :] = near[i * 128 + dz * 16:i * 128 + dz * 16 + 16, :].astype(o.dtype)
        o[32:48, :] = acc[dz * 16:(dz + 1) * 16, :].astype(o.dtype)


def scatter_blocks(order, row, act, packed, dst):
    dst[...] = jnp.zeros_like(dst)
    for k in range(0, KMAX, 2):
        @pl.when(k < order[row, GROUP])
        def _(k=k):
            r = jnp.dot(act[...], packed[:, k * DT:(k + 2) * DT], preferred_element_type=F32).astype(BF)
            dst[:, slot(order, row, k)] = r[:, :DT]

            @pl.when(k + 1 < order[row, GROUP])
            def _():
                dst[:, slot(order, row, k + 1)] = r[:, DT:]


def weight_grad_body(row, order, meta, aa, ab, tok, dst, full):
    here = slice((row - 3) * FT, (row - 2) * FT)
    join(meta, aa[here, :], ab[here, :], full)
    scatter_blocks(order, row, full, tok, dst)


def down_grad_body(order, meta, aa, ab, c0, c1, c2, c3, gd, full, cp):
    join(meta, aa[:FT, :], ab[:FT, :], full)
    for dx, c in enumerate((c0, c1, c2, c3)):
        cp[dx * 128:(dx + 1) * 128, :] = c[...]
    scatter_blocks(order, 0, full, cp, gd)


def sync(*values):
    return lax.optimization_barrier(values)


def ring_gather(v):
    up, down = [v], [v]
    for k in range(4):
        up.append(shift(up[-1], dz=1))
        if k < 3:
            down.append(shift(down[-1], dz=-1))
    return up + down[:0:-1]


class Scatter:
    def __init__(self, p):
        self.p, self.k = p, 0
        self.lo, self.hi = p[4], p[5]

    def step(self):
        k, p = self.k, self.p
        lo = shift(self.lo, dz=-1)
        hi = shift(self.hi, dz=1) if k < 3 else None
        self.k = k + 1
        if k < 3:
            self.lo = (lo.astype(F32) + p[3 - k]).astype(BF)
            self.hi = (hi.astype(F32) + p[6 + k]).astype(BF) if k < 2 else hi
            return
        self.total = p[0] + lo.astype(F32) + self.hi.astype(F32)

    def after(self, value):
        self.lo, value = sync(self.lo, value)
        return value


def local(tokens, gate_weight, up_weight, down_weight, gate_mask, up_mask, down_mask, cotangent):
    f = lax.axis_index("fsdp")
    t = lax.axis_index("tensor")
    meta = jnp.stack([f // (NX * NY), f // NY % NX, f % NY, t, t % 2]).astype(jnp.int32)

    near = shift(jnp.concatenate([tokens, cotangent], axis=0), dy=1)
    hbm = pl.BlockSpec(memory_space=pltpu.HBM)
    order = call(
        order_body,
        sds((6, GROUP + 1), jnp.int32),
        [SMEM] + [hbm] * 3,
        SMEM,
        [pltpu.SMEM((NBLK, NBLK), jnp.int32)] * 3 + [pltpu.SemaphoreType.DMA((3,))],
        mib=60,
    )(meta, gate_mask, up_mask, down_mask)
    near, order = sync(near, jnp.maximum(order, 0))
    gate_weight, up_weight = gate_weight.T, up_weight.T
    tok = jnp.concatenate([tokens, near[:8]], axis=0)
    cot = jnp.concatenate([cotangent, near[8:]], axis=0)

    wide = [tok] + [shift(tok, dx=d) for d in (1, 2, 3)]
    cot_up, cot_down = shift(cot, dz=1), shift(cot, dz=-1)
    tok_a = jnp.concatenate(wide[:2], axis=0)
    up = [shift(jnp.concatenate([tok_a, cot_up], axis=0), dz=1)]
    down = [shift(jnp.concatenate([tok_a, cot_down], axis=0), dz=-1)]
    up.append(shift(up[-1], dz=1))
    down.append(shift(down[-1], dz=-1))
    up.append(shift(up[-1], dz=1))
    down.append(shift(down[-1][:32], dz=-1))
    up.append(shift(up[-1][:32], dz=1))
    pieces_b = ring_gather(jnp.concatenate(wide[2:], axis=0))
    cots = call(
        cot_pack_body,
        tuple(sds((128, PK), BF) for _ in range(NX)),
        [SMEM] + [VMEM] * NZ,
        (VMEM,) * NX,
    )(order, cot, cot_up, up[0], up[1], up[2], down[1], down[0], cot_down)
    pieces_a = [tok_a] + up + down[::-1]
    sent = [shift(cots[d], dx=d) for d in (1, 2, 3)]
    pieces_a, pieces_b, own = sync(pieces_a, pieces_b, cots[0])
    tg, tu, keep, send = call(
        gate_up_body,
        (sds((T, PK), BF), sds((T, PK), BF), sds((2 * FT, 256), F32), sds((2 * FT, 256), F32)),
        [SMEM] * 2 + [VMEM] * (2 * NZ + 2),
        (VMEM,) * 4,
    )(order, meta, *pieces_a, *pieces_b, gate_weight, up_weight)
    cots = [own] + sent
    cots, keep, send = sync(cots, keep, send)
    sums = keep + swap_core(send)
    far = swap_far(sums.astype(BF))
    bkeep, bsend = call(
        back_body,
        (sds((FT, 256), F32), sds((FT, 256), F32)),
        [SMEM] * 2 + [VMEM] * 5,
        (VMEM,) * 2,
    )(order, meta, *cots, down_weight)
    bsums = bkeep + swap_core(bsend)
    bfar = swap_far(bsums.astype(BF))
    far, bfar = sync(far, bfar)
    acts = call(act_body, sds((3 * FT, 256), BF), [VMEM] * 4, VMEM)(sums, bsums, far, bfar)
    acts_other = swap_core(acts)
    outs = call(
        out_body,
        (sds((128, PK), F32),) + (sds((128, PK), BF),) * 3,
        [SMEM] * 2 + [VMEM] * 3,
        (VMEM,) * 4,
        [pltpu.VMEM((FT, T), BF), pltpu.VMEM((T, FT), BF)],
    )(order, meta, acts, acts_other, down_weight)
    acts, *outs = sync(acts, *outs)
    outs = [outs[0]] + [shift(outs[d], dx=-d) for d in (1, 2, 3)]
    first = (4, 5)
    near, *parts_b = call(
        tok_grad_body,
        (sds((256, W), F32),) + tuple(sds((32, W), BF if dz in first else F32) for dz in range(NZ)),
        [SMEM] * 2 + [VMEM] * 4,
        (VMEM,) * (NZ + 1),
        [pltpu.VMEM((FT, T), BF), pltpu.VMEM((T, FT), BF), pltpu.VMEM((T, FT), BF), pltpu.VMEM((256, W), F32)],
    )(order, meta, acts, acts_other, gate_weight, up_weight)
    near, outs = sync(near, outs)
    parts_a = call(
        merge_body,
        tuple(sds((48, W), BF if dz in first else F32) for dz in range(NZ)),
        [SMEM] + [VMEM] * 5,
        (VMEM,) * NZ,
        [pltpu.VMEM((128, W), F32)],
    )(order, *outs, near)

    full = pltpu.VMEM((FT, T), BF)

    def down_grad(cots):
        return call(
            down_grad_body,
            sds((FT, W), BF),
            [SMEM] * 2 + [VMEM] * 6,
            VMEM,
            [full, pltpu.VMEM((T, PK), BF)],
        )(order, meta, acts, acts_other, *cots)

    def weight_grad(row, tok):
        return call(
            functools.partial(weight_grad_body, row),
            sds((FT, W), BF),
            [SMEM] * 2 + [VMEM] * 3,
            VMEM,
            [full],
        )(order, meta, acts, acts_other, tok)

    ring_a, ring_b = Scatter(list(parts_a)), Scatter(list(parts_b))
    ring_b.step()
    cots = ring_b.after(cots)
    grad_down = down_grad(cots)
    ring_a.step()
    tg, grad_down = ring_a.after((tg, grad_down))
    grad_gate = weight_grad(4, tg)
    ring_b.step()
    ring_a.step()
    tu, grad_gate = ring_a.after((tu, grad_gate))
    grad_up = weight_grad(5, tu)
    ring_b.step()
    ring_a.step()
    grad_up = ring_a.after(grad_up)
    ring_b.step()
    ring_a.step()
    a, b = ring_a.total, ring_b.total
    mine = a[:16]
    for d, far in ((1, a[16:32]), (2, b[:16]), (3, b[16:])):
        mine = mine + shift(far.astype(BF), dx=-d).astype(F32)
    out = a[32:]
    grad_tokens = (mine[:8] + shift(mine[8:], dy=1)).astype(BF)
    ffn_output = (out[:8] + shift(out[8:], dy=1)).astype(BF)
    return (ffn_output, grad_tokens, grad_gate.T, grad_up.T, grad_down)


def solution(mesh):
    return jax.shard_map(
        local,
        mesh=mesh,
        in_specs=(
            P("fsdp", "tensor"),
            P("tensor", "fsdp"),
            P("tensor", "fsdp"),
            P("fsdp", "tensor"),
            P(),
            P(),
            P(),
            P("fsdp", "tensor"),
        ),
        out_specs=(
            P("fsdp", "tensor"),
            P("fsdp", "tensor"),
            P("tensor", "fsdp"),
            P("tensor", "fsdp"),
            P("fsdp", "tensor"),
        ),
        check_vma=False,
    )
```

```python
import functools
import jax
import jax.numpy as jnp
from jax import lax
from jax.experimental import pallas as pl
from jax.experimental.pallas import tpu as pltpu
from jax.sharding import PartitionSpec as P

NZ, NX, NY = 8, 4, 2
NBLK, GROUP, KMAX = 64, 16, 8
DT, FT = 128, 448
W = GROUP * DT
PK = KMAX * DT
T = 512
BF, F32 = jnp.bfloat16, jnp.float32
VMEM = pl.BlockSpec(memory_space=pltpu.VMEM)
SMEM = pl.BlockSpec(memory_space=pltpu.SMEM)


def fsdp_perm(dz, dx, dy):
    pairs = []
    for z in range(NZ):
        for x in range(NX):
            for y in range(NY):
                src = (z * NX + x) * NY + y
                dst = ((z + dz) % NZ * NX + (x + dx) % NX) * NY + (y + dy) % NY
                pairs.append((src, dst))
    return pairs


def shift(v, dz=0, dx=0, dy=0):
    return lax.ppermute(v, "fsdp", fsdp_perm(dz, dx, dy))


def swap_core(v):
    return lax.ppermute(v, "tensor", [(i, i ^ 1) for i in range(4)])


def swap_far(v):
    return lax.ppermute(v, "tensor", [(i, i ^ 2) for i in range(4)])


def call(body, outs, in_specs, out_specs, scratch=(), mib=20):
    return pl.pallas_call(
        body,
        out_shape=outs,
        in_specs=in_specs,
        out_specs=out_specs,
        scratch_shapes=list(scratch),
        compiler_params=pltpu.CompilerParams(vmem_limit_bytes=mib * 1024 * 1024),
        cost_estimate=pl.CostEstimate(flops=1, bytes_accessed=1, transcendentals=0),
    )


def sds(shape, dtype):
    return jax.ShapeDtypeStruct(shape, dtype)


def slot(order, row, k):
    return pl.ds(pl.multiple_of(order[row, k] * DT, DT), DT)


def order_body(meta, gm_in, um_in, dm_in, order, gm, um, dm, sem):
    loads = [
        pltpu.make_async_copy(src, dst, sem.at[i])
        for i, (src, dst) in enumerate(((gm_in, gm), (um_in, um), (dm_in, dm)))
    ]
    for load in loads:
        load.start()
    for load in loads:
        load.wait()
    z, x, y, t = meta[0], meta[1], meta[2], meta[3]
    for row in range(6):
        fx = lax.rem(x + row, NX) if row < 4 else x
        f = (z * NX + fx) * NY + y
        for k in range(KMAX + 1):
            order[row, k] = 0
        n = jnp.int32(0)
        for j in range(GROUP):
            if row < 4:
                m = dm[f, t * GROUP + j]
            elif row == 4:
                m = gm[t * GROUP + j, f]
            else:
                m = um[t * GROUP + j, f]
            order[row, n] = j
            n = n + m
        order[row, GROUP] = n


def live(order, row, k, v):
    return jnp.where(k < order[row, GROUP], v, jnp.zeros_like(v))


def pair(order, row, k, ref):
    return jnp.concatenate([ref[:, slot(order, row, k)], ref[:, slot(order, row, k + 1)]], axis=1)


COT_ROW = (0, 0, 32, 32, 32, 32, 32, 0)


def cot_pack_body(order, *refs):
    pieces, outs = refs[:NZ], refs[NZ:]
    for dx in range(NX):
        for k in range(KMAX):
            where = slot(order, dx, k)
            for dz in range(NZ):
                outs[dx][dz * 16:(dz + 1) * 16, k * DT:(k + 1) * DT] = live(
                    order, dx, k, pieces[dz][COT_ROW[dz]:COT_ROW[dz] + 16, where]
                )


def nt(a, b):
    return lax.dot_general(a, b, (((1,), (1,)), ((), ())), preferred_element_type=F32)


def gate_up_body(order, meta, *refs):
    pieces = refs[:NZ], refs[NZ:2 * NZ]
    gw, uw, tg, tu, keep, send = refs[2 * NZ:]
    for row, dst in ((4, tg), (5, tu)):
        for k in range(KMAX):
            where = slot(order, row, k)
            for dz in range(NZ):
                for dx in range(NX):
                    dst[dx * 128 + dz * 16:dx * 128 + dz * 16 + 16, k * DT:(k + 1) * DT] = live(
                        order, row, k, pieces[dx // 2][dz][dx % 2 * 16:(dx % 2 + 1) * 16, where]
                    )
    c = meta[4]
    mine = pl.ds(pl.multiple_of(c * 256, 256), 256)
    other = pl.ds(pl.multiple_of((1 - c) * 256, 256), 256)
    for rows, dst in ((other, send), (mine, keep)):
        for here, row, w, tok in ((slice(0, FT), 4, gw, tg), (slice(FT, 2 * FT), 5, uw, tu)):
            dst[here, :] = sum(
                nt(pair(order, row, k, w), tok[rows, k * DT:(k + 2) * DT]) for k in range(0, KMAX, 2)
            )


def back_body(order, meta, c0, c1, c2, c3, dw, keep, send):
    def fill(dst, a, b):
        for i, c in ((0, a), (128, b)):
            dst[:, i:i + 128] = sum(
                nt(pair(order, 0, k, dw), c[:, k * DT:(k + 2) * DT]) for k in range(0, KMAX, 2)
            )

    @pl.when(meta[4] == 0)
    def _():
        fill(send, c2, c3)
        fill(keep, c0, c1)

    @pl.when(meta[4] == 1)
    def _():
        fill(send, c0, c1)
        fill(keep, c2, c3)


def join(meta, a, b, full):
    c = meta[4]
    full[:, pl.ds(pl.multiple_of(c * 256, 256), 256)] = a
    full[:, pl.ds(pl.multiple_of((1 - c) * 256, 256), 256)] = b


def act_body(own, bown, got, bgot, acts):
    g = own[:FT, :] + got[:FT, :].astype(F32)
    u = own[FT:, :] + got[FT:, :].astype(F32)
    b = bown[...] + bgot[...].astype(F32)
    s = jax.nn.sigmoid(g)
    silu = g * s
    acts[:FT, :] = (silu * u).astype(BF)
    acts[FT:2 * FT, :] = (b * u * s * (1.0 + g * (1.0 - s))).astype(BF)
    acts[2 * FT:, :] = (b * silu).astype(BF)


def out_body(order, meta, aa, ab, dw, o0, o1, o2, o3, full, flip):
    join(meta, aa[:FT, :], ab[:FT, :], full)
    flip[...] = full[...].T
    for dx, o in ((2, o2), (1, o1), (3, o3), (0, o0)):
        for k in range(0, KMAX, 2):
            r = jnp.dot(flip[dx * 128:(dx + 1) * 128, :], pair(order, 0, k, dw), preferred_element_type=F32)
            for i in range(2):
                o[:, (k + i) * DT:(k + i + 1) * DT] = live(order, 0, k + i, r[:, i * DT:(i + 1) * DT]).astype(o.dtype)


def tok_grad_body(order, meta, aa, ab, gw, uw, near, *refs):
    outs = refs[:NZ]
    full, gflip, uflip, acc = refs[NZ:]
    join(meta, aa[FT:2 * FT, :], ab[FT:2 * FT, :], full)
    gflip[...] = full[...].T
    join(meta, aa[2 * FT:, :], ab[2 * FT:, :], full)
    uflip[...] = full[...].T
    for rows, dst in ((slice(128, T), acc), (slice(0, 128), near)):
        dst[...] = jnp.zeros_like(dst)
        for row, act, w in ((4, gflip, gw), (5, uflip, uw)):
            for k in range(0, KMAX, 2):
                r = jnp.dot(act[rows, :], pair(order, row, k, w), preferred_element_type=F32)
                for i in range(2):
                    where = slot(order, row, k + i)
                    dst[:, where] = dst[:, where] + live(order, row, k + i, r[:, i * DT:(i + 1) * DT])
    for dz in range(NZ):
        o = outs[dz]
        for i in range(3):
            o[i * 16:(i + 1) * 16, :] = acc[i * 128 + dz * 16:i * 128 + dz * 16 + 16, :].astype(o.dtype)


def merge_body(order, p0, p1, p2, p3, near, *refs):
    outs, acc = refs[:NZ], refs[NZ]
    acc[...] = jnp.zeros_like(acc)
    for dx, p in enumerate((p0, p1, p2, p3)):
        for k in range(KMAX):
            where = slot(order, dx, k)
            acc[:, where] = acc[:, where] + p[:, k * DT:(k + 1) * DT].astype(F32)
    for dz in range(NZ):
        o = outs[dz]
        o[0:16, :] = near[dz * 16:(dz + 1) * 16, :].astype(o.dtype)
        o[16:32, :] = acc[dz * 16:(dz + 1) * 16, :].astype(o.dtype)


def scatter_blocks(order, row, act, packed, dst):
    dst[...] = jnp.zeros_like(dst)
    for k in range(0, KMAX, 2):
        @pl.when(k < order[row, GROUP])
        def _(k=k):
            r = jnp.dot(act[...], packed[:, k * DT:(k + 2) * DT], preferred_element_type=F32).astype(BF)
            dst[:, slot(order, row, k)] = r[:, :DT]

            @pl.when(k + 1 < order[row, GROUP])
            def _():
                dst[:, slot(order, row, k + 1)] = r[:, DT:]


def weight_grad_body(row, order, meta, aa, ab, tok, dst, full):
    here = slice((row - 3) * FT, (row - 2) * FT)
    join(meta, aa[here, :], ab[here, :], full)
    scatter_blocks(order, row, full, tok, dst)


def down_grad_body(order, meta, aa, ab, c0, c1, c2, c3, gd, full, cp):
    join(meta, aa[:FT, :], ab[:FT, :], full)
    for dx, c in enumerate((c0, c1, c2, c3)):
        cp[dx * 128:(dx + 1) * 128, :] = c[...]
    scatter_blocks(order, 0, full, cp, gd)


def sync(*values):
    return lax.optimization_barrier(values)


def ring_gather(v):
    up, down = [v], [v]
    for k in range(4):
        up.append(shift(up[-1], dz=1))
        if k < 3:
            down.append(shift(down[-1], dz=-1))
    return up + down[:0:-1]


class Scatter:
    def __init__(self, p):
        self.p, self.k = p, 0
        self.lo, self.hi = p[4], p[5]

    def step(self):
        k, p = self.k, self.p
        lo = shift(self.lo, dz=-1)
        hi = shift(self.hi, dz=1) if k < 3 else None
        self.k = k + 1
        if k < 3:
            self.lo = (lo.astype(F32) + p[3 - k]).astype(BF)
            self.hi = (hi.astype(F32) + p[6 + k]).astype(BF) if k < 2 else hi
            return
        self.total = p[0] + lo.astype(F32) + self.hi.astype(F32)

    def after(self, value):
        self.lo, value = sync(self.lo, value)
        return value


def local(tokens, gate_weight, up_weight, down_weight, gate_mask, up_mask, down_mask, cotangent):
    f = lax.axis_index("fsdp")
    t = lax.axis_index("tensor")
    meta = jnp.stack([f // (NX * NY), f // NY % NX, f % NY, t, t % 2]).astype(jnp.int32)

    near = shift(jnp.concatenate([tokens, cotangent], axis=0), dy=1)
    hbm = pl.BlockSpec(memory_space=pltpu.HBM)
    order = call(
        order_body,
        sds((6, GROUP + 1), jnp.int32),
        [SMEM] + [hbm] * 3,
        SMEM,
        [pltpu.SMEM((NBLK, NBLK), jnp.int32)] * 3 + [pltpu.SemaphoreType.DMA((3,))],
        mib=60,
    )(meta, gate_mask, up_mask, down_mask)
    near, order = sync(near, jnp.maximum(order, 0))
    gate_weight, up_weight = gate_weight.T, up_weight.T
    tok = jnp.concatenate([tokens, near[:8]], axis=0)
    cot = jnp.concatenate([cotangent, near[8:]], axis=0)

    wide = [tok] + [shift(tok, dx=d) for d in (1, 2, 3)]
    cot_up, cot_down = shift(cot, dz=1), shift(cot, dz=-1)
    tok_a = jnp.concatenate(wide[:2], axis=0)
    up = [shift(jnp.concatenate([tok_a, cot_up], axis=0), dz=1)]
    down = [shift(jnp.concatenate([tok_a, cot_down], axis=0), dz=-1)]
    up.append(shift(up[-1], dz=1))
    down.append(shift(down[-1], dz=-1))
    up.append(shift(up[-1], dz=1))
    down.append(shift(down[-1][:32], dz=-1))
    up.append(shift(up[-1][:32], dz=1))
    pieces_b = ring_gather(jnp.concatenate(wide[2:], axis=0))
    cots = call(
        cot_pack_body,
        tuple(sds((128, PK), BF) for _ in range(NX)),
        [SMEM] + [VMEM] * NZ,
        (VMEM,) * NX,
    )(order, cot, cot_up, up[0], up[1], up[2], down[1], down[0], cot_down)
    pieces_a = [tok_a] + up + down[::-1]
    sent = [shift(cots[d], dx=d) for d in (1, 2, 3)]
    pieces_a, pieces_b, own = sync(pieces_a, pieces_b, cots[0])
    tg, tu, keep, send = call(
        gate_up_body,
        (sds((T, PK), BF), sds((T, PK), BF), sds((2 * FT, 256), F32), sds((2 * FT, 256), F32)),
        [SMEM] * 2 + [VMEM] * (2 * NZ + 2),
        (VMEM,) * 4,
    )(order, meta, *pieces_a, *pieces_b, gate_weight, up_weight)
    cots = [own] + sent
    cots, keep, send = sync(cots, keep, send)
    sums = keep + swap_core(send)
    far = swap_far(sums.astype(BF))
    bkeep, bsend = call(
        back_body,
        (sds((FT, 256), F32), sds((FT, 256), F32)),
        [SMEM] * 2 + [VMEM] * 5,
        (VMEM,) * 2,
    )(order, meta, *cots, down_weight)
    bsums = bkeep + swap_core(bsend)
    bfar = swap_far(bsums.astype(BF))
    far, bfar = sync(far, bfar)
    acts = call(act_body, sds((3 * FT, 256), BF), [VMEM] * 4, VMEM)(sums, bsums, far, bfar)
    acts_other = swap_core(acts)
    outs = call(
        out_body,
        (sds((128, PK), F32),) + (sds((128, PK), BF),) * 3,
        [SMEM] * 2 + [VMEM] * 3,
        (VMEM,) * 4,
        [pltpu.VMEM((FT, T), BF), pltpu.VMEM((T, FT), BF)],
    )(order, meta, acts, acts_other, down_weight)
    acts, *outs = sync(acts, *outs)
    outs = [outs[0]] + [shift(outs[d], dx=-d) for d in (1, 2, 3)]
    first = (4, 5)
    near, *parts_b = call(
        tok_grad_body,
        (sds((128, W), F32),) + tuple(sds((48, W), BF if dz in first else F32) for dz in range(NZ)),
        [SMEM] * 2 + [VMEM] * 4,
        (VMEM,) * (NZ + 1),
        [pltpu.VMEM((FT, T), BF), pltpu.VMEM((T, FT), BF), pltpu.VMEM((T, FT), BF), pltpu.VMEM((384, W), F32)],
    )(order, meta, acts, acts_other, gate_weight, up_weight)
    near, outs = sync(near, outs)
    parts_a = call(
        merge_body,
        tuple(sds((32, W), BF if dz in first else F32) for dz in range(NZ)),
        [SMEM] + [VMEM] * 5,
        (VMEM,) * NZ,
        [pltpu.VMEM((128, W), F32)],
    )(order, *outs, near)

    full = pltpu.VMEM((FT, T), BF)

    def down_grad(cots):
        return call(
            down_grad_body,
            sds((FT, W), BF),
            [SMEM] * 2 + [VMEM] * 6,
            VMEM,
            [full, pltpu.VMEM((T, PK), BF)],
        )(order, meta, acts, acts_other, *cots)

    def weight_grad(row, tok):
        return call(
            functools.partial(weight_grad_body, row),
            sds((FT, W), BF),
            [SMEM] * 2 + [VMEM] * 3,
            VMEM,
            [full],
        )(order, meta, acts, acts_other, tok)

    ring_a, ring_b = Scatter(list(parts_a)), Scatter(list(parts_b))
    ring_b.step()
    cots = ring_b.after(cots)
    grad_down = down_grad(cots)
    ring_a.step()
    tg, grad_down = ring_a.after((tg, grad_down))
    grad_gate = weight_grad(4, tg)
    ring_b.step()
    ring_a.step()
    tu, grad_gate = ring_a.after((tu, grad_gate))
    grad_up = weight_grad(5, tu)
    ring_b.step()
    ring_a.step()
    grad_up = ring_a.after(grad_up)
    ring_b.step()
    ring_a.step()
    a, b = ring_a.total, ring_b.total
    mine = a[:16]
    for d, far in ((1, b[:16]), (2, b[16:32]), (3, b[32:])):
        mine = mine + shift(far.astype(BF), dx=-d).astype(F32)
    out = a[16:]
    grad_tokens = (mine[:8] + shift(mine[8:], dy=1)).astype(BF)
    ffn_output = (out[:8] + shift(out[8:], dy=1)).astype(BF)
    return (ffn_output, grad_tokens, grad_gate.T, grad_up.T, grad_down)


def solution(mesh):
    return jax.shard_map(
        local,
        mesh=mesh,
        in_specs=(
            P("fsdp", "tensor"),
            P("tensor", "fsdp"),
            P("tensor", "fsdp"),
            P("fsdp", "tensor"),
            P(),
            P(),
            P(),
            P("fsdp", "tensor"),
        ),
        out_specs=(
            P("fsdp", "tensor"),
            P("fsdp", "tensor"),
            P("tensor", "fsdp"),
            P("tensor", "fsdp"),
            P("fsdp", "tensor"),
        ),
        check_vma=False,
    )
```
